32 devices in a mesh: vox: 8 (over y, x, core), chan: 4 (over z).
Axes of the slice: x: 2, y: 2, z: 4, core: 2. Of those that a mesh axis runs over, the one named last changes fastest.
Arguments:
- activations: bfloat16 [1024, 8, 512], P('chan', 'vox'), may hold values from -6 to 6
- upstream: bfloat16 [512, 8, 512], P('chan', 'vox'), may hold values from -6 to 6
- weights: bfloat16 [512, 27, 1024], P('chan'), may hold values from -0.0390625 to 0.0390625
Outputs:
- outputs: bfloat16 [512, 8, 512], P('chan', 'vox')
- input_grad: bfloat16 [1024, 8, 512], P('chan', 'vox')
- weight_grad: bfloat16 [512, 27, 1024], P('chan')
The draws below stay inside these ranges and needn't reach their ends.
All inputs are finite; a program needn't handle non-finite values.
Results may differ from the reference program's by a relative error of at most 0.001.
Values may be sent and summed in bfloat16 or wider, within the bound.
A program may use at most 192 MiB of HBM per device.

```python
import jax
import jax.numpy as jnp

CIN = 1024
COUT = 512
NY = 32
NZ = 16
NX = 8


def level_of(stream_key, shape, shards, least, high):
    def one(dim, blocks):
        heights = jax.random.uniform(jax.random.fold_in(jax.random.fold_in(stream_key, 6), dim), (blocks,), jnp.float32, least / len(shards), high / len(shards))
        return jnp.repeat(jnp.exp(heights), shape[dim] // blocks).reshape((-1,) + (1,) * (len(shape) - dim - 1))

    gain = one(*shards[0])
    for cut in shards[1:]:
        gain = gain * one(*cut)
    return gain


def scatter_about(own_key, extent, deviation, most, split=(), kind=jnp.bfloat16):
    values = jax.random.normal(own_key, extent, jnp.float32) * deviation
    if len(split) > 0:
        values = level_of(own_key, extent, split, -0.22, 0.18) * values
    return jnp.clip(values, min=-most, max=most).astype(kind)


def setup_inputs(seed: int = 0) -> dict:
    key_of = jax.random.split(jax.random.key(seed), 4)
    activations = scatter_about(key_of[0], (CIN, NX, NY * NZ), 1.0, 6.0, ((0, 4), (1, 8)))
    upstream = scatter_about(key_of[1], (COUT, NX, NY * NZ), 1.0, 6.0, ((0, 4), (1, 8)))
    weights = scatter_about(key_of[2], (COUT, 27, CIN), (27 * CIN) ** -0.5, 0.0390625, ((0, 4),))
    return dict(activations=activations, upstream=upstream, weights=weights)


tap_offsets = [(a, b, c) for a in (-1, 0, 1) for b in (-1, 0, 1) for c in (-1, 0, 1)]

def shifted(volume, off_x, off_y, off_z):
    channels = volume.shape[0]
    padded = jnp.pad(volume.reshape(channels, NX, NY, NZ), ((0, 0), (1, 1), (1, 1), (1, 1)))
    window = padded[:, 1 + off_x:1 + off_x + NX, 1 + off_y:1 + off_y + NY, 1 + off_z:1 + off_z + NZ]
    return window.reshape(channels, NX * NY * NZ)

def reference(activations, upstream, weights):
    up_flat = upstream.reshape(COUT, NX * NY * NZ)
    out_total = jnp.zeros((COUT, NX * NY * NZ), jnp.float32)
    grad_total = jnp.zeros((CIN, NX * NY * NZ), jnp.float32)
    weight_terms = []
    for index, offsets in enumerate(tap_offsets):
        moved = shifted(activations, offsets[0], offsets[1], offsets[2])
        back = shifted(upstream, -offsets[0], -offsets[1], -offsets[2])
        tap_weight = weights[:, index, :]
        out_total = out_total + jnp.dot(tap_weight, moved, preferred_element_type=jnp.float32)
        grad_total = grad_total + jnp.dot(tap_weight.T, back, preferred_element_type=jnp.float32)
        weight_terms.append(jnp.dot(up_flat, moved.T, preferred_element_type=jnp.float32))
    raw_grad = jnp.stack(weight_terms, axis=1)
    grad_scale = 1.0 / jnp.sqrt(jnp.float32(NX * NY * NZ))
    outputs = out_total.reshape(COUT, NX, NY * NZ).astype(jnp.bfloat16)
    input_grad = grad_total.reshape(CIN, NX, NY * NZ).astype(jnp.bfloat16)
    weight_grad = (raw_grad * grad_scale).astype(jnp.bfloat16)
    return (outputs, input_grad, weight_grad)
```

```python
import jax
import jax.numpy as jnp
from jax import lax
from jax.experimental import pallas as pl
from jax.experimental.pallas import tpu as pltpu
from jax.sharding import PartitionSpec as P

NY = 32
NZ = 16
PLANE = NY * NZ

in_plane = [(b, c) for b in (-1, 0, 1) for c in (-1, 0, 1)]


def moved(value, off_y, off_z):
    if off_y == 0 and off_z == 0:
        return value
    spot = lax.broadcasted_iota(jnp.int32, value.shape, 1)
    row, lane = spot // NZ + off_y, spot % NZ + off_z
    keep = (row >= 0) & (row < NY) & (lane >= 0) & (lane < NZ)
    turned = pltpu.roll(value, (-(off_y * NZ + off_z)) % PLANE, 1)
    return jnp.where(keep, turned, 0.0)


def back_kernel(up_ref, out_ref):
    for a in (-1, 0, 1):
        value = up_ref[1 - a].astype(jnp.float32)
        for t, (b, c) in enumerate(in_plane):
            out_ref[a + 1, t] = moved(value, -b, -c).astype(jnp.bfloat16)


def fold_kernel(z_ref, out_ref):
    total = jnp.zeros(out_ref.shape, jnp.float32)
    for t, (b, c) in enumerate(in_plane):
        total = total + moved(z_ref[t], b, c)
    out_ref[...] = total.astype(out_ref.dtype)


def wgrad_kernel(scale, up_ref, act_ref, out_ref, shifts, total):
    planes, rows = up_ref.shape[0], up_ref.shape[1]
    total[...] = jnp.zeros_like(total)

    @pl.loop(0, planes)
    def _(u):
        value = up_ref[u].astype(jnp.float32)
        for t, (b, c) in enumerate(in_plane):
            shifts[pl.ds(t * rows, rows), :] = moved(value, -b, -c).astype(jnp.bfloat16)
        for a in (-1, 0, 1):

            @pl.when((u + a >= 0) & (u + a < planes))
            def _():
                total[a + 1] += lax.dot_general(
                    shifts[...], act_ref[u + a], (((1,), (1,)), ((), ())), preferred_element_type=jnp.float32
                )

    for a in range(3):
        for t in range(9):
            out_ref[a * 9 + t] = (total[a, pl.ds(t * rows, rows), :] * scale).astype(jnp.bfloat16)


VMEM = pl.BlockSpec(memory_space=pltpu.VMEM)


def call(kernel, shape, dtype, flops, moved_bytes, limit, scratch=()):
    return pl.pallas_call(
        kernel,
        out_shape=jax.ShapeDtypeStruct(shape, dtype),
        out_specs=VMEM,
        scratch_shapes=list(scratch),
        compiler_params=pltpu.CompilerParams(vmem_limit_bytes=limit),
        cost_estimate=pl.CostEstimate(flops=flops, bytes_accessed=moved_bytes, transcendentals=0),
    )


def local(activations, upstream, weights):
    cin_dev = activations.shape[0]
    rows = upstream.shape[0]
    cin = weights.shape[2]
    vox, chan = lax.axis_size("vox"), lax.axis_size("chan")
    me = lax.axis_index("vox")
    half_id = me % 2
    half = cin // 2
    scale = (vox * activations.shape[1] * PLANE) ** -0.5
    pairs = [(i, i ^ 1) for i in range(vox)]
    act = activations.reshape(cin_dev, PLANE)
    up = upstream.reshape(rows, PLANE)

    panel = lax.all_gather(act, "chan", axis=0, tiled=True)
    up_all = lax.all_gather(up, "vox", axis=0, tiled=False)

    blank = jnp.zeros((1, rows, PLANE), jnp.bfloat16)
    up_near = lax.dynamic_slice_in_dim(jnp.concatenate([blank, up_all, blank]), me, 3, axis=0)
    back = call(back_kernel, (3, 9, rows, PLANE), jnp.bfloat16, 27 * rows * PLANE * 8, 30 * rows * PLANE * 2, 32 << 20)(up_near)
    part = jnp.einsum(
        "okc,kov->cv", weights, back.reshape(27, rows, PLANE), preferred_element_type=jnp.float32
    )
    input_grad = lax.psum_scatter(part, "chan", scatter_dimension=0, tiled=True)
    input_grad = input_grad.astype(jnp.bfloat16).reshape(cin_dev, 1, PLANE)

    other = lax.ppermute(lax.dynamic_slice_in_dim(panel, (1 - half_id) * half, half, axis=0), "vox", pairs)
    own = lax.dynamic_slice_in_dim(panel, half_id * half, half, axis=0)
    even = half_id == 0
    two = jnp.stack([jnp.where(even, own, other), jnp.where(even, other, own)])
    groups = [list(range(0, vox, 2)), list(range(1, vox, 2))]
    act_half = lax.all_gather(two, "vox", axis=0, tiled=True, axis_index_groups=groups)

    before = lax.ppermute(panel, "vox", [(i, i + 1) for i in range(vox - 1)])
    after = lax.ppermute(panel, "vox", [(i + 1, i) for i in range(vox - 1)])
    near = jnp.stack([before, panel, after])
    parts = jnp.einsum(
        "oabi,aip->bop", weights.reshape(rows, 3, 9, cin), near, preferred_element_type=jnp.float32
    )
    outputs = call(fold_kernel, (rows, PLANE), jnp.bfloat16, 9 * rows * PLANE * 8, 10 * rows * PLANE * 4, 32 << 20)(parts)
    outputs = outputs.reshape(rows, 1, PLANE)

    mine = call(
        lambda *refs: wgrad_kernel(scale, *refs),
        (27, rows, half),
        jnp.bfloat16,
        2 * 27 * rows * half * vox * PLANE,
        2 * (vox * PLANE * (rows + half) + 27 * rows * half),
        56 << 20,
        [pltpu.VMEM((9 * rows, PLANE), jnp.bfloat16), pltpu.VMEM((3, 9 * rows, half), jnp.float32)],
    )(up_all, act_half)
    theirs = lax.ppermute(mine, "vox", pairs)
    low, high = jnp.where(even, mine, theirs), jnp.where(even, theirs, mine)
    weight_grad = jnp.concatenate([low, high], axis=2).transpose(1, 0, 2)
    return outputs, input_grad, weight_grad


def solution(mesh):
    return jax.shard_map(
        local,
        mesh=mesh,
        in_specs=(P("chan", "vox", None), P("chan", "vox", None), P("chan", None, None)),
        out_specs=(P("chan", "vox", None), P("chan", "vox", None), P("chan", None, None)),
        check_vma=False,
    )
```

```python
import jax
import jax.numpy as jnp
from jax import lax
from jax.experimental import pallas as pl
from jax.experimental.pallas import tpu as pltpu
from jax.sharding import PartitionSpec as P

NY = 32
NZ = 16
PLANE = NY * NZ

in_plane = [(b, c) for b in (-1, 0, 1) for c in (-1, 0, 1)]


def moved(value, off_y, off_z):
    if off_y == 0 and off_z == 0:
        return value
    spot = lax.broadcasted_iota(jnp.int32, value.shape, 1)
    row, lane = spot // NZ + off_y, spot % NZ + off_z
    keep = (row >= 0) & (row < NY) & (lane >= 0) & (lane < NZ)
    turned = pltpu.roll(value, (-(off_y * NZ + off_z)) % PLANE, 1)
    return jnp.where(keep, turned, 0.0)


def back_kernel(up_ref, out_ref):
    for a in (-1, 0, 1):
        value = up_ref[1 - a].astype(jnp.float32)
        for t, (b, c) in enumerate(in_plane):
            out_ref[a + 1, t] = moved(value, -b, -c).astype(jnp.bfloat16)


def fold_kernel(z_ref, out_ref):
    total = jnp.zeros(out_ref.shape, jnp.float32)
    for t, (b, c) in enumerate(in_plane):
        total = total + moved(z_ref[t], b, c)
    out_ref[...] = total.astype(out_ref.dtype)


def flipped(index, step, size):
    result, bit = 0, 1
    while bit < size:
        result = result + bit * ((index // bit + step // bit) % 2)
        bit *= 2
    return result


def wgrad_kernel(
    scale, vox, chan, act_ref, up_ref, out_ref, near_ref, pass_ref,
    panel, up_all, act_half, shifts, total,
    z_send, z_recv, up_send, up_recv, act_send, act_recv,
):
    me, z = lax.axis_index("vox"), lax.axis_index("chan")
    cin_dev, rows = act_ref.shape[0], up_ref.shape[0]
    side, spot = me % 2, me // 2
    blocks = chan // 2

    barrier = pltpu.get_barrier_semaphore()
    for d in range(1, chan):
        pl.semaphore_signal(barrier, inc=1, device_id=(me, flipped(z, d, chan)), device_id_type=pl.DeviceIdType.MESH)
    for d in range(1, vox):
        pl.semaphore_signal(barrier, inc=1, device_id=(flipped(me, d, vox), z), device_id_type=pl.DeviceIdType.MESH)
    pl.semaphore_wait(barrier, chan + vox - 2)

    def z_copy(d, source):
        return pltpu.make_async_remote_copy(
            src_ref=act_ref, dst_ref=panel.at[source], send_sem=z_send.at[d], recv_sem=z_recv.at[source],
            device_id=(me, flipped(z, d, chan)), device_id_type=pl.DeviceIdType.MESH,
        )

    def up_copy(d, source):
        return pltpu.make_async_remote_copy(
            src_ref=up_ref, dst_ref=up_all.at[source], send_sem=up_send.at[d], recv_sem=up_recv.at[source],
            device_id=(flipped(me, d, vox), z), device_id_type=pl.DeviceIdType.MESH,
        )

    def act_copy(block, d, source, target):
        place = block % blocks
        return pltpu.make_async_remote_copy(
            src_ref=panel.at[block],
            dst_ref=act_half.at[source, pl.ds(pl.multiple_of(place * cin_dev, cin_dev), cin_dev)],
            send_sem=act_send.at[block, d], recv_sem=act_recv.at[source, place],
            device_id=(target, z), device_id_type=pl.DeviceIdType.MESH,
        )

    def each_target(block, act):
        part = block // blocks
        for d in range(vox // 2):
            target = 2 * flipped(spot, d, vox // 2) + part
            if d == 0:

                @pl.when(part != side)
                def _():
                    act(act_copy(block, d, me, target))
            else:
                act(act_copy(block, d, me, target))

    for d in range(1, chan):
        z_copy(d, z).start()
    panel[z] = act_ref[...]
    each_target(z, lambda copy: copy.start())
    for d in range(1, vox):
        up_copy(d, me).start()
    up_all[me] = up_ref[...]
    total[...] = jnp.zeros_like(total)
    for d in range(1, chan):
        source = flipped(z, d, chan)
        z_copy(d, source).wait_recv()
        each_target(source, lambda copy: copy.start())

    @pl.loop(0, blocks)
    def _(place):
        at = pl.multiple_of(place * cin_dev, cin_dev)
        act_half[me, pl.ds(at, cin_dev), :] = panel[side * blocks + place]

    @pl.loop(0, vox)
    def _(d):
        u = flipped(me, d, vox)

        @pl.when(d > 0)
        def _():
            up_copy(d, u).wait_recv()

        value = up_all[u].astype(jnp.float32)
        for t, (b, c) in enumerate(in_plane):
            shifts[u, pl.ds(t * rows, rows), :] = moved(value, -b, -c).astype(jnp.bfloat16)

    @pl.loop(0, vox)
    def _(d):
        x = flipped(me, d, vox)

        @pl.when(d > 0)
        def _():
            for place in range(blocks):
                act_copy(place, 0, x, me).wait_recv()

        for a in (-1, 0, 1):

            @pl.when((x - a >= 0) & (x - a < vox))
            def _():
                total[a + 1] += lax.dot_general(
                    shifts[x - a], act_half[x], (((1,), (1,)), ((), ())), preferred_element_type=jnp.float32
                )

    for ref, centre in ((near_ref, me), (pass_ref, flipped(me, 1, vox))):
        for a in (-1, 0, 1):
            inside = (centre + a >= 0) & (centre + a < vox)

            @pl.when(inside)
            def _():
                ref[a + 1] = act_half[centre + a]

            @pl.when(jnp.logical_not(inside))
            def _():
                ref[a + 1] = jnp.zeros(ref.shape[1:], ref.dtype)

    for a in range(3):
        for t in range(9):
            out_ref[a * 9 + t] = (total[a, pl.ds(t * rows, rows), :] * scale).astype(jnp.bfloat16)

    for d in range(1, chan):
        z_copy(d, z).wait_send()
    for d in range(1, vox):
        up_copy(d, me).wait_send()
    for d in range(chan):
        each_target(flipped(z, d, chan), lambda copy: copy.wait_send())


def join_kernel(mine_ref, theirs_ref, out_ref, sems):
    half = mine_ref.shape[2]
    side = lax.axis_index("vox") % 2
    copies = [
        pltpu.make_async_copy(
            ref, out_ref.at[:, :, pl.ds(pl.multiple_of(place * half, half), half)], sems.at[n]
        )
        for n, (ref, place) in enumerate(((mine_ref, side), (theirs_ref, 1 - side)))
    ]
    for copy in copies:
        copy.start()
    for copy in copies:
        copy.wait()


VMEM = pl.BlockSpec(memory_space=pltpu.VMEM)


def call(kernel, shape, dtype, flops, moved_bytes, limit, scratch=()):
    return pl.pallas_call(
        kernel,
        out_shape=jax.ShapeDtypeStruct(shape, dtype),
        out_specs=VMEM,
        scratch_shapes=list(scratch),
        compiler_params=pltpu.CompilerParams(vmem_limit_bytes=limit),
        cost_estimate=pl.CostEstimate(flops=flops, bytes_accessed=moved_bytes, transcendentals=0),
    )


def local(activations, upstream, weights):
    cin_dev = activations.shape[0]
    rows = upstream.shape[0]
    cin = weights.shape[2]
    vox, chan = lax.axis_size("vox"), lax.axis_size("chan")
    even = lax.axis_index("vox") % 2 == 0
    half = cin // 2
    scale = (vox * activations.shape[1] * PLANE) ** -0.5
    pairs = [(i, i ^ 1) for i in range(vox)]
    act = activations.reshape(cin_dev, PLANE)
    up = upstream.reshape(rows, PLANE)

    below = lax.ppermute(up, "vox", [(i, i + 1) for i in range(vox - 1)])
    above = lax.ppermute(up, "vox", [(i + 1, i) for i in range(vox - 1)])
    up_near = jnp.stack([below, up, above])
    back = call(back_kernel, (3, 9, rows, PLANE), jnp.bfloat16, 27 * rows * PLANE * 8, 30 * rows * PLANE * 2, 32 << 20)(up_near)
    part = jnp.einsum(
        "okc,kov->cv", weights, back.reshape(27, rows, PLANE), preferred_element_type=jnp.float32
    )
    act, part = lax.optimization_barrier((act, part))
    input_grad = lax.psum_scatter(part, "chan", scatter_dimension=0, tiled=True)
    input_grad = input_grad.astype(jnp.bfloat16).reshape(cin_dev, 1, PLANE)

    dma = pltpu.SemaphoreType.DMA
    mine, near, passed = pl.pallas_call(
        lambda *refs: wgrad_kernel(scale, vox, chan, *refs),
        out_shape=(
            jax.ShapeDtypeStruct((27, rows, half), jnp.bfloat16),
            jax.ShapeDtypeStruct((3, half, PLANE), jnp.bfloat16),
            jax.ShapeDtypeStruct((3, half, PLANE), jnp.bfloat16),
        ),
        in_specs=[VMEM, VMEM],
        out_specs=(VMEM, VMEM, VMEM),
        scratch_shapes=[
            pltpu.VMEM((chan, cin_dev, PLANE), jnp.bfloat16),
            pltpu.VMEM((vox, rows, PLANE), jnp.bfloat16),
            pltpu.VMEM((vox, half, PLANE), jnp.bfloat16),
            pltpu.VMEM((vox, 9 * rows, PLANE), jnp.bfloat16),
            pltpu.VMEM((3, 9 * rows, half), jnp.float32),
            dma((chan,)),
            dma((chan,)),
            dma((vox,)),
            dma((vox,)),
            dma((chan, vox // 2)),
            dma((vox, chan // 2)),
        ],
        compiler_params=pltpu.CompilerParams(
            vmem_limit_bytes=56 << 20, collective_id=0, has_side_effects=True
        ),
        cost_estimate=pl.CostEstimate(
            flops=4 * 27 * rows * half * vox * PLANE,
            bytes_accessed=2 * (PLANE * (rows + cin_dev + 6 * half) + 27 * rows * half),
            transcendentals=0,
        ),
    )(act, up)

    rest = lax.ppermute(passed, "vox", pairs)
    theirs = lax.ppermute(mine, "vox", pairs)
    full = jnp.concatenate([jnp.where(even, near, rest), jnp.where(even, rest, near)], axis=1)
    parts = jnp.einsum(
        "oabi,aip->bop", weights.reshape(rows, 3, 9, cin), full, preferred_element_type=jnp.float32
    )
    outputs = call(fold_kernel, (rows, PLANE), jnp.bfloat16, 9 * rows * PLANE * 8, 10 * rows * PLANE * 4, 32 << 20)(parts)
    outputs = outputs.reshape(rows, 1, PLANE)

    anywhere = pl.BlockSpec(memory_space=pl.ANY)
    weight_grad = pl.pallas_call(
        join_kernel,
        out_shape=jax.ShapeDtypeStruct((27, rows, cin), jnp.bfloat16),
        in_specs=[anywhere, anywhere],
        out_specs=anywhere,
        scratch_shapes=[dma((2,))],
        cost_estimate=pl.CostEstimate(flops=0, bytes_accessed=4 * 27 * rows * cin, transcendentals=0),
    )(mine, theirs)
    return outputs, input_grad, weight_grad.transpose(1, 0, 2)


def solution(mesh):
    return jax.shard_map(
        local,
        mesh=mesh,
        in_specs=(P("chan", "vox", None), P("chan", "vox", None), P("chan", None, None)),
        out_specs=(P("chan", "vox", None), P("chan", "vox", None), P("chan", None, None)),
        check_vma=False,
    )
```

```python
import jax
import jax.numpy as jnp
from jax import lax
from jax.experimental import pallas as pl
from jax.experimental.pallas import tpu as pltpu
from jax.sharding import PartitionSpec as P

NY = 32
NZ = 16
PLANE = NY * NZ

in_plane = [(b, c) for b in (-1, 0, 1) for c in (-1, 0, 1)]


def moved(value, off_y, off_z):
    if off_y == 0 and off_z == 0:
        return value
    spot = lax.broadcasted_iota(jnp.int32, value.shape, 1)
    row, lane = spot // NZ + off_y, spot % NZ + off_z
    keep = (row >= 0) & (row < NY) & (lane >= 0) & (lane < NZ)
    turned = pltpu.roll(value, (-(off_y * NZ + off_z)) % PLANE, 1)
    return jnp.where(keep, turned, 0.0)


def back_kernel(up_ref, out_ref):
    for a in (-1, 0, 1):
        value = up_ref[1 - a].astype(jnp.float32)
        for t, (b, c) in enumerate(in_plane):
            out_ref[a + 1, t] = moved(value, -b, -c).astype(jnp.bfloat16)


def fold_kernel(z_ref, out_ref):
    total = jnp.zeros(out_ref.shape, jnp.float32)
    for t, (b, c) in enumerate(in_plane):
        total = total + moved(z_ref[t], b, c)
    out_ref[...] = total.astype(out_ref.dtype)


def flipped(index, step, size):
    result, bit = 0, 1
    while bit < size:
        result = result + bit * ((index // bit + step // bit) % 2)
        bit *= 2
    return result


def wgrad_kernel(
    scale, vox, chan, act_ref, up_ref, out_ref, near_ref, pass_ref,
    panel, up_all, act_half, shifts, total,
    z_send, z_recv, up_send, up_recv, act_send, act_recv,
):
    me, z = lax.axis_index("vox"), lax.axis_index("chan")
    cin_dev, rows = act_ref.shape[0], up_ref.shape[0]
    side, spot = me % 2, me // 2
    blocks = chan // 2

    barrier = pltpu.get_barrier_semaphore()
    for d in range(1, chan):
        pl.semaphore_signal(barrier, inc=1, device_id=(me, flipped(z, d, chan)), device_id_type=pl.DeviceIdType.MESH)
    for d in range(1, vox):
        pl.semaphore_signal(barrier, inc=1, device_id=(flipped(me, d, vox), z), device_id_type=pl.DeviceIdType.MESH)
    pl.semaphore_wait(barrier, chan + vox - 2)

    def z_copy(d, source):
        return pltpu.make_async_remote_copy(
            src_ref=act_ref, dst_ref=panel.at[source], send_sem=z_send.at[d], recv_sem=z_recv.at[source],
            device_id=(me, flipped(z, d, chan)), device_id_type=pl.DeviceIdType.MESH,
        )

    def up_copy(d, source):
        return pltpu.make_async_remote_copy(
            src_ref=up_ref, dst_ref=up_all.at[source], send_sem=up_send.at[d], recv_sem=up_recv.at[source],
            device_id=(flipped(me, d, vox), z), device_id_type=pl.DeviceIdType.MESH,
        )

    def act_copy(block, d, source, target):
        place = block % blocks
        return pltpu.make_async_remote_copy(
            src_ref=panel.at[block],
            dst_ref=act_half.at[source, pl.ds(pl.multiple_of(place * cin_dev, cin_dev), cin_dev)],
            send_sem=act_send.at[block, d], recv_sem=act_recv.at[source, place],
            device_id=(target, z), device_id_type=pl.DeviceIdType.MESH,
        )

    def each_target(block, act):
        part = block // blocks
        for d in range(vox // 2):
            target = 2 * flipped(spot, d, vox // 2) + part
            if d == 0:

                @pl.when(part != side)
                def _():
                    act(act_copy(block, d, me, target))
            else:
                act(act_copy(block, d, me, target))

    for d in range(1, chan):
        z_copy(d, z).start()
    panel[z] = act_ref[...]
    each_target(z, lambda copy: copy.start())
    for d in range(1, vox):
        up_copy(d, me).start()
    up_all[me] = up_ref[...]
    total[...] = jnp.zeros_like(total)
    for d in range(1, chan):
        source = flipped(z, d, chan)
        z_copy(d, source).wait_recv()
        each_target(source, lambda copy: copy.start())

    @pl.loop(0, blocks)
    def _(place):
        at = pl.multiple_of(place * cin_dev, cin_dev)
        act_half[me, pl.ds(at, cin_dev), :] = panel[side * blocks + place]

    @pl.loop(0, vox)
    def _(d):
        u = flipped(me, d, vox)

        @pl.when(d > 0)
        def _():
            up_copy(d, u).wait_recv()

        value = up_all[u].astype(jnp.float32)
        for t, (b, c) in enumerate(in_plane):
            shifts[u, pl.ds(t * rows, rows), :] = moved(value, -b, -c).astype(jnp.bfloat16)

    @pl.loop(0, vox)
    def _(d):
        x = flipped(me, d, vox)

        @pl.when(d > 0)
        def _():
            for place in range(blocks):
                act_copy(place, 0, x, me).wait_recv()

        for a in (-1, 0, 1):

            @pl.when((x - a >= 0) & (x - a < vox))
            def _():
                total[a + 1] += lax.dot_general(
                    shifts[x - a], act_half[x], (((1,), (1,)), ((), ())), preferred_element_type=jnp.float32
                )

    for ref, centre in ((near_ref, me), (pass_ref, flipped(me, 1, vox))):
        for a in (-1, 0, 1):
            inside = (centre + a >= 0) & (centre + a < vox)

            @pl.when(inside)
            def _():
                ref[a + 1] = act_half[centre + a]

            @pl.when(jnp.logical_not(inside))
            def _():
                ref[a + 1] = jnp.zeros(ref.shape[1:], ref.dtype)

    for a in range(3):
        for t in range(9):
            out_ref[a * 9 + t] = (total[a, pl.ds(t * rows, rows), :] * scale).astype(jnp.bfloat16)

    for d in range(1, chan):
        z_copy(d, z).wait_send()
    for d in range(1, vox):
        up_copy(d, me).wait_send()
    for d in range(chan):
        each_target(flipped(z, d, chan), lambda copy: copy.wait_send())


def join_kernel(mine_ref, theirs_ref, out_ref):
    half = mine_ref.shape[2]
    side = lax.axis_index("vox") % 2
    for place in (0, 1):

        @pl.when(side == place)
        def _():
            out_ref[:, :, place * half : (place + 1) * half] = mine_ref[...]
            out_ref[:, :, (1 - place) * half : (2 - place) * half] = theirs_ref[...]


VMEM = pl.BlockSpec(memory_space=pltpu.VMEM)


def call(kernel, shape, dtype, flops, moved_bytes, limit, scratch=()):
    return pl.pallas_call(
        kernel,
        out_shape=jax.ShapeDtypeStruct(shape, dtype),
        out_specs=VMEM,
        scratch_shapes=list(scratch),
        compiler_params=pltpu.CompilerParams(vmem_limit_bytes=limit),
        cost_estimate=pl.CostEstimate(flops=flops, bytes_accessed=moved_bytes, transcendentals=0),
    )


def local(activations, upstream, weights):
    cin_dev = activations.shape[0]
    rows = upstream.shape[0]
    cin = weights.shape[2]
    vox, chan = lax.axis_size("vox"), lax.axis_size("chan")
    even = lax.axis_index("vox") % 2 == 0
    half = cin // 2
    scale = (vox * activations.shape[1] * PLANE) ** -0.5
    pairs = [(i, i ^ 1) for i in range(vox)]
    act = activations.reshape(cin_dev, PLANE)
    up = upstream.reshape(rows, PLANE)

    below = lax.ppermute(up, "vox", [(i, i + 1) for i in range(vox - 1)])
    above = lax.ppermute(up, "vox", [(i + 1, i) for i in range(vox - 1)])
    up_near = jnp.stack([below, up, above])
    back = call(back_kernel, (3, 9, rows, PLANE), jnp.bfloat16, 27 * rows * PLANE * 8, 30 * rows * PLANE * 2, 32 << 20)(up_near)
    part = jnp.einsum(
        "okc,kov->cv", weights, back.reshape(27, rows, PLANE), preferred_element_type=jnp.float32
    )
    act, part = lax.optimization_barrier((act, part))
    input_grad = lax.psum_scatter(part, "chan", scatter_dimension=0, tiled=True)
    input_grad = input_grad.astype(jnp.bfloat16).reshape(cin_dev, 1, PLANE)

    dma = pltpu.SemaphoreType.DMA
    mine, near, passed = pl.pallas_call(
        lambda *refs: wgrad_kernel(scale, vox, chan, *refs),
        out_shape=(
            jax.ShapeDtypeStruct((27, rows, half), jnp.bfloat16),
            jax.ShapeDtypeStruct((3, half, PLANE), jnp.bfloat16),
            jax.ShapeDtypeStruct((3, half, PLANE), jnp.bfloat16),
        ),
        in_specs=[VMEM, VMEM],
        out_specs=(VMEM, VMEM, VMEM),
        scratch_shapes=[
            pltpu.VMEM((chan, cin_dev, PLANE), jnp.bfloat16),
            pltpu.VMEM((vox, rows, PLANE), jnp.bfloat16),
            pltpu.VMEM((vox, half, PLANE), jnp.bfloat16),
            pltpu.VMEM((vox, 9 * rows, PLANE), jnp.bfloat16),
            pltpu.VMEM((3, 9 * rows, half), jnp.float32),
            dma((chan,)),
            dma((chan,)),
            dma((vox,)),
            dma((vox,)),
            dma((chan, vox // 2)),
            dma((vox, chan // 2)),
        ],
        compiler_params=pltpu.CompilerParams(
            vmem_limit_bytes=56 << 20, collective_id=0, has_side_effects=True
        ),
        cost_estimate=pl.CostEstimate(
            flops=4 * 27 * rows * half * vox * PLANE,
            bytes_accessed=2 * (PLANE * (rows + cin_dev + 6 * half) + 27 * rows * half),
            transcendentals=0,
        ),
    )(act, up)

    rest = lax.ppermute(passed, "vox", pairs)
    theirs = lax.ppermute(mine, "vox", pairs)
    full = jnp.concatenate([jnp.where(even, near, rest), jnp.where(even, rest, near)], axis=1)
    parts = jnp.einsum(
        "oabi,aip->bop", weights.reshape(rows, 3, 9, cin), full, preferred_element_type=jnp.float32
    )
    outputs = call(fold_kernel, (rows, PLANE), jnp.bfloat16, 9 * rows * PLANE * 8, 10 * rows * PLANE * 4, 32 << 20)(parts)
    outputs = outputs.reshape(rows, 1, PLANE)

    part_spec = pl.BlockSpec((3, rows, half), lambda n: (n, 0, 0))
    weight_grad = pl.pallas_call(
        join_kernel,
        grid=(9,),
        out_shape=jax.ShapeDtypeStruct((27, rows, cin), jnp.bfloat16),
        in_specs=[part_spec, part_spec],
        out_specs=pl.BlockSpec((3, rows, cin), lambda n: (n, 0, 0)),
        compiler_params=pltpu.CompilerParams(vmem_limit_bytes=32 << 20),
        cost_estimate=pl.CostEstimate(flops=0, bytes_accessed=4 * 27 * rows * cin, transcendentals=0),
    )(mine, theirs)
    return outputs, input_grad, weight_grad.transpose(1, 0, 2)


def solution(mesh):
    return jax.shard_map(
        local,
        mesh=mesh,
        in_specs=(P("chan", "vox", None), P("chan", "vox", None), P("chan", None, None)),
        out_specs=(P("chan", "vox", None), P("chan", "vox", None), P("chan", None, None)),
        check_vma=False,
    )
```
